256 devices in a mesh: mem: 4 (over z_hi), tile: 64 (over y, z_lo, x, core).
Axes of the slice: x: 4, y: 4, z: 8 (z_hi: 4, z_lo: 2; z = z_hi * 2 + z_lo), core: 2. Of those that a mesh axis runs over, the one named last changes fastest.
Arguments:
- alpha: float32 [32, 8, 1536, 384], P('mem', None, 'tile'), may hold values from -6 to 6
- ensemble: bfloat16 [2, 32, 8, 1536, 384], P(None, 'mem', None, 'tile'), may hold values from -1 to 1
- innovation: float32 [2, 8, 1536, 384], P(None, None, 'tile'), may hold values from -6 to 6
- precision: float32 [2, 8, 1536, 384], P(None, None, 'tile'), may hold values from 0.5 to 8
- diffusivity: float32 [2, 8, 1536, 384], P(None, None, 'tile'), may hold values from 0.01 to 0.48, as said below
Outputs:
- gradient: float32 [32, 8, 1536, 384], P('mem', None, 'tile')
- increment: float32 [2, 8, 1536, 384], P(None, None, 'tile')
The draws below stay inside these ranges and needn't reach their ends.
Inputs may be any that keep to these rules, and one draw needn't show every extreme that they name: diffusivity[0] lies between 0.40 and 0.48 and diffusivity[1] between 0.01 and 0.02, so the four faces of a cell sum to at most 1.
All inputs are finite; a program needn't handle non-finite values.
Results may differ from the reference program's by a relative error of at most 0.0003.
Values sent between devices are 32-bit elements; how exact they have to be, the bound alone decides.
No kernel may reach another device: no remote copies, remote signals or barrier semaphores. Data moves between devices by JAX's collectives and lax.ppermute only.
A program may use at most 64 MiB of HBM per device.

```python
import math
import jax
import jax.numpy as jnp
from jax import lax

NROW = 384
LEVELS = 8
SLOTS = 2
STEPS = 4
MEMBERS = 32
NCOL = 1536


def draw_diffusivity(key, part):
    zonal_key = jax.random.fold_in(key, 101)
    merid_key = jax.random.fold_in(key, 202)
    zonal_low = 0.4
    zonal = jax.random.uniform(zonal_key, (1, LEVELS, NCOL, NROW), jnp.float32, zonal_low, 0.48)
    merid = jax.random.uniform(merid_key, (1, LEVELS, NCOL, NROW), jnp.float32, 0.01, 0.02)
    return jnp.concatenate([zonal, merid], axis=0)


def block_levels(own_key, dims, pieces, smallest, high):
    def one(position, parts):
        heights = jax.random.uniform(jax.random.fold_in(jax.random.fold_in(own_key, 6), position), (parts,), jnp.float32, smallest / len(pieces), high / len(pieces))
        return jnp.repeat(jnp.exp(heights), dims[position] // parts).reshape((-1,) + (1,) * (len(dims) - position - 1))

    level = one(*pieces[0])
    for cut in pieces[1:]:
        level = level * one(*cut)
    return level


def scatter_about(own_key, shape, scale, reach, cuts=(), kind=jnp.bfloat16):
    loudness = block_levels(own_key, shape, cuts, -0.22, 0.18) if cuts else 1.0
    entries = jax.random.normal(own_key, shape, jnp.float32) * scale * loudness
    return jnp.minimum(jnp.maximum(entries, -reach), reach).astype(kind)


def setup_inputs(seed: int = 0) -> dict:
    keys = jax.random.split(jax.random.key(seed), 6)
    return {
        "alpha": scatter_about(keys[0], (MEMBERS, LEVELS, NCOL, NROW), 1.0, 6.0, ((0, 4), (2, 64)), jnp.float32),
        "ensemble": scatter_about(keys[1], (SLOTS, MEMBERS, LEVELS, NCOL, NROW), MEMBERS ** -0.5, 1.0, ((1, 4), (3, 64))),
        "innovation": scatter_about(keys[2], (SLOTS, LEVELS, NCOL, NROW), 1.0, 6.0, ((2, 64),), jnp.float32),
        "precision": jnp.clip(jnp.exp(math.log(8.0) - 2.7725887 * jax.random.uniform(keys[3], (SLOTS, LEVELS, NCOL, NROW), jnp.float32) ** block_levels(keys[3], (SLOTS, LEVELS, NCOL, NROW), ((2, 64),), -0.2, 0.2)), 0.5, 8.0),
        "diffusivity": draw_diffusivity(jax.random.fold_in(keys[5], 71), 0),
    }


def diffuse_step(field, diffusivity):
    east = jnp.roll(field, -1, axis=1)
    zonal_flux = diffusivity[0] * (east - field)
    merid_flux = diffusivity[1][:, :, :-1] * (field[:, :, 1:] - field[:, :, :-1])
    padding = jnp.zeros_like(field[:, :, :1])
    north_flux = jnp.concatenate([merid_flux, padding], axis=2)
    south_flux = jnp.concatenate([padding, merid_flux], axis=2)
    return field + zonal_flux - jnp.roll(zonal_flux, 1, axis=1) + north_flux - south_flux

def localize(field, diffusivity):
    for sweep in range(STEPS):
        field = diffuse_step(field, diffusivity)
    return field

def reference(alpha, ensemble, innovation, precision, diffusivity):
    members_first = jnp.swapaxes(ensemble, 0, 1)

    def accumulate(total, items):
        control, perturb = items
        localized = localize(control, diffusivity)
        return (total + perturb.astype(jnp.float32) * localized[None], None)
    start = jnp.zeros(innovation.shape, jnp.float32)
    increment, unused = lax.scan(accumulate, start, (alpha, members_first))
    weighted = precision * (increment - innovation)

    def member_grad(items):
        control, perturb = items
        projected = lax.optimization_barrier(jnp.sum(perturb.astype(jnp.float32) * weighted, axis=0))
        return control + localize(projected, diffusivity)
    gradient = lax.map(member_grad, (alpha, members_first))
    return (gradient, increment)
```

```python
import jax
import jax.numpy as jnp
from jax import lax
from jax.experimental import pallas as pl
from jax.experimental.pallas import tpu as pltpu
from jax.sharding import PartitionSpec as P

STEPS = 4
HALO = 4
TILE_ROWS = 8
VMEM_BYTES = 48 * 1024 * 1024


def shifted(values, by, axis):
    return pltpu.roll(values, by % values.shape[axis], axis)


def low_half(shape):
    return lax.broadcasted_iota(jnp.int32, shape, len(shape) - 2) < HALO


def masked_rows(face):
    last = lax.broadcasted_iota(jnp.int32, face.shape, 1) == face.shape[1] - 1
    return jnp.where(last, 0.0, face)


def diffuse(field, zonal, merid):
    for sweep in range(STEPS):
        zonal_flux = zonal * (shifted(field, -1, 0) - field)
        merid_flux = merid * (shifted(field, -1, 1) - field)
        field = field + (zonal_flux - shifted(zonal_flux, 1, 0))
        field = field + (merid_flux - shifted(merid_flux, 1, 1))
    return field


def paired_heads(first, second):
    return jnp.where(low_half(first.shape), first, shifted(second, HALO, 0))


def paired_tails(first, second):
    return jnp.where(low_half(first.shape), shifted(first, HALO, 0), second)


def halo_tiles(from_left, from_right):
    low = low_half(from_left.shape)
    first = jnp.where(low, from_right, shifted(from_left, HALO, 0))
    second = jnp.where(low, shifted(from_right, HALO, 0), from_left)
    return first, second


def pack_controls(alpha_lo, alpha_hi, coeffs_lo, coeffs_hi, head, tail):
    members = alpha_lo.shape[0]
    for m in range(members):
        head[m, 0] = paired_heads(alpha_lo[m, 0], alpha_lo[m, 1])
        tail[m, 0] = paired_tails(alpha_hi[m, 0], alpha_hi[m, 1])
    for f in range(2):
        head[members + f, 0] = paired_heads(coeffs_lo[f, 0], coeffs_lo[f, 1])
        tail[members + f, 0] = paired_tails(coeffs_hi[f, 0], coeffs_hi[f, 1])


def pack_ensemble(ensemble, head, tail):
    slots, members = ensemble.shape[:2]

    def one(m, carry):
        for t in range(slots):
            first = ensemble[t, m, 0].astype(jnp.float32)
            second = ensemble[t, m, 1].astype(jnp.float32)
            head[t, m, 0] = paired_heads(first[:8], second[:8])
            tail[t, m, 0] = paired_tails(first[16:], second[16:])
        return carry

    lax.fori_loop(0, members, one, 0)


def localize_interior(alpha, ensemble, coeffs, out):
    members = alpha.shape[0]
    zonal = coeffs[0, 0]
    merid = masked_rows(coeffs[1, 0])
    low = low_half((TILE_ROWS, alpha.shape[3]))

    def one(m, sums):
        field = diffuse(alpha[m, 0], zonal, merid)
        return tuple(
            total + ensemble[t, m, 0].astype(jnp.float32) * field for t, total in enumerate(sums)
        )

    zero = jnp.zeros(alpha.shape[2:], jnp.float32)
    sums = lax.fori_loop(0, members, one, (zero, zero))
    for t, total in enumerate(sums):
        out[t, 0, :8] = total[8:16]
        out[t, 0, 8:] = jnp.where(low, total[16:], total[:8])


def edge_slabs(hi, lo, left, right):
    first, second = halo_tiles(left, right)
    return (
        jnp.concatenate([hi[0], first, lo[0]], axis=0),
        jnp.concatenate([hi[1], second, lo[1]], axis=0),
    )


def edge_coeffs(coeffs_lo, coeffs_hi, left, right, base):
    zonal = edge_slabs(coeffs_hi[0], coeffs_lo[0], left[base, 0], right[base, 0])
    merid = edge_slabs(coeffs_hi[1], coeffs_lo[1], left[base + 1, 0], right[base + 1, 0])
    return zonal, tuple(masked_rows(face) for face in merid)


def localize_edges(alpha_lo, alpha_hi, ensemble, coeffs_lo, coeffs_hi, left, right, out):
    members = alpha_lo.shape[0]
    zonal, merid = edge_coeffs(coeffs_lo, coeffs_hi, left, right, members)
    low = low_half((TILE_ROWS, out.shape[3]))

    def one(m, sums):
        slabs = edge_slabs(alpha_hi[m], alpha_lo[m], left[m, 0], right[m, 0])
        new = []
        for j in range(2):
            field = diffuse(slabs[j], zonal[j], merid[j])
            edge = jnp.where(low, field[16:], field[:8])
            for t in range(2):
                scale = ensemble[t, m, j].astype(jnp.float32)
                new.append(sums[2 * j + t] + jnp.where(low, scale[:8], scale[16:]) * edge)
        return tuple(new)

    zero = jnp.zeros(out.shape[2:], jnp.float32)
    sums = lax.fori_loop(0, members, one, (zero,) * 4)
    for j in range(2):
        for t in range(2):
            out[t, j] = sums[2 * j + t]


def weigh_edges(mine, other, innov_lo, innov_hi, prec_lo, prec_hi, head, tail):
    low = low_half((TILE_ROWS, mine.shape[3]))
    for t in range(2):
        edges = []
        for j in range(2):
            innovation = jnp.where(low, innov_lo[t, j], innov_hi[t, j])
            precision = jnp.where(low, prec_lo[t, j], prec_hi[t, j])
            edges.append(precision * (mine[t, j] + other[t, j] - innovation))
        head[t, 0] = paired_heads(edges[0], edges[1])
        tail[t, 0] = paired_tails(edges[0], edges[1])


def adjoint_interior(
    mine, other, mine_edge, other_edge, innovation, precision, ensemble, alpha, coeffs,
    increment, weighted, inner,
):
    members = alpha.shape[0]
    low = low_half((TILE_ROWS, alpha.shape[3]))
    zonal = coeffs[0, 0]
    merid = masked_rows(coeffs[1, 0])
    weights = []
    for t in range(2):
        middle = mine[t, 0] + other[t, 0]
        edge = mine_edge[t, 0] + other_edge[t, 0]
        rest = middle[8:]
        total = jnp.concatenate(
            [jnp.where(low, edge, rest), middle[:8], jnp.where(low, rest, edge)], axis=0
        )
        increment[t, 0] = total
        weights.append(precision[t, 0] * (total - innovation[t, 0]))
        weighted[t, 0] = weights[t]

    def one(m, carry):
        projected = ensemble[0, m, 0].astype(jnp.float32) * weights[0]
        projected = projected + ensemble[1, m, 0].astype(jnp.float32) * weights[1]
        inner[m, 0] = alpha[m, 0] + diffuse(projected, zonal, merid)
        return carry

    lax.fori_loop(0, members, one, 0)


def adjoint_edges(
    inner, alpha_lo, alpha_hi, ensemble, ens_left, ens_right, weighted, w_left, w_right,
    coeffs_lo, coeffs_hi, left, right, gradient,
):
    members = inner.shape[0]
    low = low_half((TILE_ROWS, inner.shape[3]))
    zonal, merid = edge_coeffs(coeffs_lo, coeffs_hi, left, right, members)

    def one(m, carry):
        halo_left = ens_left[0, m, 0] * w_left[0, 0] + ens_left[1, m, 0] * w_left[1, 0]
        halo_right = ens_right[0, m, 0] * w_right[0, 0] + ens_right[1, m, 0] * w_right[1, 0]
        halos = halo_tiles(halo_left, halo_right)
        for j in range(2):
            projected = ensemble[0, m, j].astype(jnp.float32) * weighted[0, j]
            projected = projected + ensemble[1, m, j].astype(jnp.float32) * weighted[1, j]
            slab = jnp.concatenate([projected[16:], halos[j], projected[:8]], axis=0)
            field = diffuse(slab, zonal[j], merid[j])
            gradient[m, j, :8] = jnp.where(low, alpha_lo[m, j] + field[16:], inner[m, j, :8])
            gradient[m, j, 8:16] = inner[m, j, 8:16]
            gradient[m, j, 16:] = jnp.where(low, inner[m, j, 16:], alpha_hi[m, j] + field[:8])
        return carry

    lax.fori_loop(0, members, one, 0)


def block(shape, dims, at=0):
    walk, step = dims
    sizes = tuple(step if d == walk else n for d, n in enumerate(shape))
    return pl.BlockSpec(sizes, lambda i: tuple(i if d == walk else 0 for d in range(len(shape))))


def rows8(shape, dims, at):
    walk, step = dims
    sizes = tuple(step if d == walk else n for d, n in enumerate(shape[:2 + len(shape) - 4]))
    sizes = sizes + (TILE_ROWS, shape[-1])
    last = len(shape) - 2
    return pl.BlockSpec(
        sizes, lambda i: tuple(i if d == walk else at if d == last else 0 for d in range(len(shape)))
    )


def f32(*shape):
    return jax.ShapeDtypeStruct(shape, jnp.float32)


def run(kernel, grid, in_specs, out_specs, out_shape, flops, *args):
    read = sum(a.size * a.dtype.itemsize for a in args)
    wrote = sum(4 * s.size for s in jax.tree.leaves(out_shape))
    return pl.pallas_call(
        kernel,
        grid=(grid,),
        in_specs=in_specs,
        out_specs=out_specs,
        out_shape=out_shape,
        cost_estimate=pl.CostEstimate(flops=flops, bytes_accessed=read + wrote, transcendentals=0),
        compiler_params=pltpu.CompilerParams(vmem_limit_bytes=VMEM_BYTES),
    )(*args)


def to_right(value):
    size = lax.axis_size("tile")
    return lax.ppermute(value, "tile", [(i, (i + 1) % size) for i in range(size)])


def to_left(value):
    size = lax.axis_size("tile")
    return lax.ppermute(value, "tile", [(i, (i - 1) % size) for i in range(size)])


def with_partner(value, first):
    mem, tile = lax.axis_size("mem"), lax.axis_size("tile")
    pairs = []
    for m in range(mem):
        for t in range(tile):
            flip = 1 if (t % 2 == 0) == first else 3
            pairs.append((m * tile + t, (m ^ flip) * tile + t))
    return lax.ppermute(value, ("mem", "tile"), pairs)


def per_device(alpha, ensemble, innovation, precision, diffusivity):
    members, levels, columns, rows = alpha.shape
    slots = ensemble.shape[0]
    pairs = levels // 2
    work = members * levels * columns * rows * 10 * STEPS

    a_lo, a_hi = (rows8(alpha.shape, (1, 2), at) for at in (0, 2))
    c_lo, c_hi = (rows8(diffusivity.shape, (1, 2), at) for at in (0, 2))
    edge = f32(members + 2, pairs, TILE_ROWS, rows)
    edge_spec = block(edge.shape, (1, 1))
    head, tail = run(
        pack_controls, pairs, [a_lo, a_hi, c_lo, c_hi], [edge_spec] * 2, [edge] * 2, 0,
        alpha, alpha, diffusivity, diffusivity,
    )
    left = to_right(tail)
    right = to_left(head)

    mid = f32(slots, levels, 16, rows)
    part_mid = run(
        localize_interior, levels,
        [block(alpha.shape, (1, 1)), block(ensemble.shape, (2, 1)), block(diffusivity.shape, (1, 1))],
        block(mid.shape, (1, 1)), mid, work, alpha, ensemble, diffusivity,
    )
    got_mid = with_partner(part_mid, True)

    ens_edge = f32(slots, members, pairs, TILE_ROWS, rows)
    ens_edge_spec = block(ens_edge.shape, (2, 1))
    ens_head, ens_tail = run(
        pack_ensemble, pairs, [block(ensemble.shape, (2, 2))], [ens_edge_spec] * 2, [ens_edge] * 2, 0,
        ensemble,
    )

    rim = f32(slots, levels, TILE_ROWS, rows)
    part_rim = run(
        localize_edges, pairs,
        [a_lo, a_hi, block(ensemble.shape, (2, 2)), c_lo, c_hi, edge_spec, edge_spec],
        block(rim.shape, (1, 2)), rim, work,
        alpha, alpha, ensemble, diffusivity, diffusivity, left, right,
    )
    got_rim = with_partner(part_rim, True)
    half_mid = part_mid + got_mid
    other_mid = with_partner(half_mid, False)
    half_rim = part_rim + got_rim
    other_rim = with_partner(half_rim, False)
    ens_left = to_right(ens_tail)
    ens_right = to_left(ens_head)

    o_lo, o_hi = (rows8(innovation.shape, (1, 2), at) for at in (0, 2))
    w_edge = f32(slots, pairs, TILE_ROWS, rows)
    w_edge_spec = block(w_edge.shape, (1, 1))
    rim_spec = block(rim.shape, (1, 2))
    w_head, w_tail = run(
        weigh_edges, pairs, [rim_spec, rim_spec, o_lo, o_hi, o_lo, o_hi],
        [w_edge_spec] * 2, [w_edge] * 2, 0,
        half_rim, other_rim, innovation, innovation, precision, precision,
    )
    w_left = to_right(w_tail)
    w_right = to_left(w_head)

    obs = f32(*innovation.shape)
    obs_spec = block(obs.shape, (1, 1))
    mid_spec, rim1_spec = block(mid.shape, (1, 1)), block(rim.shape, (1, 1))
    field = f32(*alpha.shape)
    field_spec = block(alpha.shape, (1, 1))
    increment, weighted, inner = run(
        adjoint_interior, levels,
        [mid_spec, mid_spec, rim1_spec, rim1_spec, obs_spec, obs_spec,
         block(ensemble.shape, (2, 1)), field_spec, block(diffusivity.shape, (1, 1))],
        [obs_spec, obs_spec, field_spec], [obs, obs, field], work,
        half_mid, other_mid, half_rim, other_rim, innovation, precision, ensemble, alpha, diffusivity,
    )

    field2_spec = block(alpha.shape, (1, 2))
    gradient = run(
        adjoint_edges, pairs,
        [field2_spec, a_lo, a_hi, block(ensemble.shape, (2, 2)), ens_edge_spec, ens_edge_spec,
         block(obs.shape, (1, 2)), w_edge_spec, w_edge_spec, c_lo, c_hi, edge_spec, edge_spec],
        field2_spec, field, work,
        inner, alpha, alpha, ensemble, ens_left, ens_right, weighted, w_left, w_right,
        diffusivity, diffusivity, left, right,
    )
    return (gradient, increment)


def solution(mesh):
    in_specs = (
        P("mem", None, "tile", None),
        P(None, "mem", None, "tile", None),
        P(None, None, "tile", None),
        P(None, None, "tile", None),
        P(None, None, "tile", None),
    )
    out_specs = (P("mem", None, "tile", None), P(None, None, "tile", None))
    return jax.shard_map(
        per_device, mesh=mesh, in_specs=in_specs, out_specs=out_specs, check_vma=False
    )
```

```python
import jax
import jax.numpy as jnp
from jax import lax
from jax.experimental import pallas as pl
from jax.experimental.pallas import tpu as pltpu
from jax.sharding import PartitionSpec as P

STEPS = 4
HALO = 4
TILE_ROWS = 8
VMEM_BYTES = 48 * 1024 * 1024


def shifted(values, by, axis):
    return pltpu.roll(values, by % values.shape[axis], axis)


def low_half(shape):
    return lax.broadcasted_iota(jnp.int32, shape, len(shape) - 2) < HALO


def masked_rows(face):
    last = lax.broadcasted_iota(jnp.int32, face.shape, 1) == face.shape[1] - 1
    return jnp.where(last, 0.0, face)


def diffuse(fields, zonal, merid):
    rows = lax.broadcasted_iota(jnp.int32, (TILE_ROWS, zonal.shape[1]), 0)
    kept = [None] * len(fields)
    for sweep in range(STEPS):
        zonal_flux = [zonal * (shifted(f, -1, 0) - f) for f in fields]
        merid_flux = [merid * (shifted(f, -1, 1) - f) for f in fields]
        inward = [shifted(z, 1, 0) for z in zonal_flux]
        for i, f in enumerate(fields):
            cell = jnp.where(rows < HALO, f[:8], f[16:])
            flux = jnp.where(rows < HALO, zonal_flux[i][:8], inward[i][16:])
            if sweep:
                mine = (rows == sweep) | (rows == 7 - sweep)
                cell = jnp.where(mine, cell, kept[i][0])
                flux = jnp.where(mine, flux, kept[i][1])
            kept[i] = (cell, flux)
        fields = [
            (f + (z - w)) + (g - shifted(g, 1, 1))
            for f, z, w, g in zip(fields, zonal_flux, inward, merid_flux)
        ]
    return fields, kept


def window(outer, inner, by, side):
    if by == 0:
        return outer
    rows = lax.broadcasted_iota(jnp.int32, outer.shape, 0) % HALO
    if side == 0:
        return jnp.where(rows < HALO - by, shifted(outer, -by, 0), shifted(inner, HALO - by, 0))
    return jnp.where(rows >= by, shifted(outer, by, 0), shifted(inner, by - HALO, 0))


def edge_windows(outer, own, side):
    zonal_at = 0 if side == 0 else 1
    steps = []
    for step in range(STEPS):
        zonal = window(outer[0], own[0], step + zonal_at, side)
        merid = window(outer[1], own[1], step + 1, side)
        steps.append((zonal, masked_rows(merid)))
    return steps


def diffuse_edges(halos, kept, windows, side):
    rows = lax.broadcasted_iota(jnp.int32, halos[0].shape, 0) % HALO
    inward = -1 if side == 0 else 1
    newest = rows == (HALO - 1 if side == 0 else 0)
    outer = halos
    for step in range(STEPS):
        zonal, merid = windows[step]
        turn = -inward * (HALO - 1 - step)
        cells, flux_in = [], []
        for previous, (cell, flux) in zip(outer, kept):
            cells.append(jnp.where(newest, shifted(cell, turn, 0), shifted(previous, inward, 0)))
            flux_in.append(shifted(flux, turn, 0))
        merid_flux = [merid * (shifted(c, -1, 1) - c) for c in cells]
        after = []
        for previous, cell, flux, g in zip(outer, cells, flux_in, merid_flux):
            out_flux = zonal * (cell - previous if side == 0 else previous - cell)
            in_flux = jnp.where(newest, flux, shifted(out_flux, inward, 0))
            change = in_flux - out_flux if side == 0 else out_flux - in_flux
            after.append((cell + change) + (g - shifted(g, 1, 1)))
        outer = after
    return outer


def paired_heads(first, second):
    return jnp.where(low_half(first.shape), first, shifted(second, HALO, 0))


def paired_tails(first, second):
    return jnp.where(low_half(first.shape), shifted(first, HALO, 0), second)


def paired(first, second, side):
    return (paired_heads if side == 0 else paired_tails)(first, second)


def levels_of(left, right):
    low = low_half(left.shape)
    return (
        jnp.where(low, left, shifted(right, HALO, 0)),
        jnp.where(low, shifted(left, HALO, 0), right),
    )


def pack_controls(alpha_lo, alpha_hi, coeffs_lo, coeffs_hi, head, tail):
    members = alpha_lo.shape[0]
    for m in range(members):
        head[m, 0] = paired_heads(alpha_lo[m, 0], alpha_lo[m, 1])
        tail[m, 0] = paired_tails(alpha_hi[m, 0], alpha_hi[m, 1])
    for f in range(2):
        head[members + f, 0] = paired_heads(coeffs_lo[f, 0], coeffs_lo[f, 1])
        tail[members + f, 0] = paired_tails(coeffs_hi[f, 0], coeffs_hi[f, 1])


def pack_ensemble(ensemble, head, tail):
    slots, members = ensemble.shape[:2]

    def one(m, carry):
        for t in range(slots):
            first = ensemble[t, m, 0].astype(jnp.float32)
            second = ensemble[t, m, 1].astype(jnp.float32)
            head[t, m, 0] = paired_heads(first[:8], second[:8])
            tail[t, m, 0] = paired_tails(first[16:], second[16:])
        return carry

    lax.fori_loop(0, members, one, 0)


def keep_all(kept, cells, fluxes):
    for m, (cell, flux) in enumerate(kept):
        cells[m, 0] = cell
        fluxes[m, 0] = flux


def localize_interior(alpha, ensemble, coeffs, out, cells, fluxes):
    members = alpha.shape[0]
    low = low_half((TILE_ROWS, alpha.shape[3]))
    fields = [alpha[m, 0] for m in range(members)]
    fields, kept = diffuse(fields, coeffs[0, 0], masked_rows(coeffs[1, 0]))
    keep_all(kept, cells, fluxes)
    for t in range(2):
        total = ensemble[t, 0, 0].astype(jnp.float32) * fields[0]
        for m in range(1, members):
            total = total + ensemble[t, m, 0].astype(jnp.float32) * fields[m]
        out[t, 0, :8] = total[8:16]
        out[t, 0, 8:] = jnp.where(low, total[16:], total[:8])


def edges_of(halos, cells, fluxes, coeffs_lo, coeffs_hi, outer, base, members, side):
    own = coeffs_lo if side == 0 else coeffs_hi
    own = [paired(own[f, 0], own[f, 1], side) for f in range(2)]
    windows = edge_windows([outer[base, 0], outer[base + 1, 0]], own, side)
    kept = [
        (paired(cells[m, 0], cells[m, 1], side), paired(fluxes[m, 0], fluxes[m, 1], side))
        for m in range(members)
    ]
    return diffuse_edges([halos[m, 0] for m in range(members)], kept, windows, side)


def localize_edges(
    left, right, cells, fluxes, coeffs_lo, coeffs_hi, ens_head, ens_tail, out,
):
    members = cells.shape[0]
    for side, (outer, scale) in enumerate(((left, ens_head), (right, ens_tail))):
        edges = edges_of(
            outer, cells, fluxes, coeffs_lo, coeffs_hi, outer, members, members, side
        )
        for t in range(2):
            total = scale[t, 0, 0] * edges[0]
            for m in range(1, members):
                total = total + scale[t, m, 0] * edges[m]
            out[t, side, 0] = total


def project_edges(
    mine, other, innov_lo, innov_hi, prec_lo, prec_hi, ens_head, ens_tail, rim, head, tail
):
    members = ens_head.shape[1]
    totals = [[mine[t, side, 0] + other[t, side, 0] for side in range(2)] for t in range(2)]
    for t in range(2):
        first, second = levels_of(*totals[t])
        rim[t, 0] = first
        rim[t, 1] = second
    sides = ((innov_lo, prec_lo, ens_head, head), (innov_hi, prec_hi, ens_tail, tail))
    for side, (innov, prec, scale, out) in enumerate(sides):
        weights = [
            paired(prec[t, 0], prec[t, 1], side)
            * (totals[t][side] - paired(innov[t, 0], innov[t, 1], side))
            for t in range(2)
        ]
        for m in range(members):
            out[m, 0] = scale[0, m, 0] * weights[0] + scale[1, m, 0] * weights[1]


def adjoint_interior(
    mine, other, rim, innovation, precision, ensemble, alpha, coeffs,
    increment, inner, cells, fluxes,
):
    members = alpha.shape[0]
    low = low_half((TILE_ROWS, alpha.shape[3]))
    weights = []
    for t in range(2):
        middle = mine[t, 0] + other[t, 0]
        edge, rest = rim[t, 0], middle[8:]
        total = jnp.concatenate(
            [jnp.where(low, edge, rest), middle[:8], jnp.where(low, rest, edge)], axis=0
        )
        increment[t, 0] = total
        weights.append(precision[t, 0] * (total - innovation[t, 0]))
    projected = [
        ensemble[0, m, 0].astype(jnp.float32) * weights[0]
        + ensemble[1, m, 0].astype(jnp.float32) * weights[1]
        for m in range(members)
    ]
    fields, kept = diffuse(projected, coeffs[0, 0], masked_rows(coeffs[1, 0]))
    keep_all(kept, cells, fluxes)
    for m in range(members):
        inner[m, 0] = alpha[m, 0] + fields[m]


def adjoint_edges(
    inner, alpha_lo, alpha_hi, p_left, p_right, cells, fluxes, coeffs_lo, coeffs_hi, left, right,
    gradient,
):
    members = inner.shape[0]
    low = low_half((TILE_ROWS, inner.shape[3]))
    sides = [
        edges_of(halos, cells, fluxes, coeffs_lo, coeffs_hi, outer, members, members, side)
        for side, (halos, outer) in enumerate(((p_left, left), (p_right, right)))
    ]
    for m in range(members):
        for j, edge in enumerate(levels_of(sides[0][m], sides[1][m])):
            gradient[m, j, :8] = jnp.where(low, alpha_lo[m, j] + edge, inner[m, j, :8])
            gradient[m, j, 8:16] = inner[m, j, 8:16]
            gradient[m, j, 16:] = jnp.where(low, inner[m, j, 16:], alpha_hi[m, j] + edge)


def block(shape, dims, at=0):
    walk, step = dims
    sizes = tuple(step if d == walk else n for d, n in enumerate(shape))
    return pl.BlockSpec(sizes, lambda i: tuple(i if d == walk else 0 for d in range(len(shape))))


def rows8(shape, dims, at):
    walk, step = dims
    sizes = tuple(step if d == walk else n for d, n in enumerate(shape[:2 + len(shape) - 4]))
    sizes = sizes + (TILE_ROWS, shape[-1])
    last = len(shape) - 2
    return pl.BlockSpec(
        sizes, lambda i: tuple(i if d == walk else at if d == last else 0 for d in range(len(shape)))
    )


def f32(*shape):
    return jax.ShapeDtypeStruct(shape, jnp.float32)


def run(kernel, grid, in_specs, out_specs, out_shape, flops, *args):
    read = sum(a.size * a.dtype.itemsize for a in args)
    wrote = sum(4 * s.size for s in jax.tree.leaves(out_shape))
    return pl.pallas_call(
        kernel,
        grid=(grid,),
        in_specs=in_specs,
        out_specs=out_specs,
        out_shape=out_shape,
        cost_estimate=pl.CostEstimate(flops=flops, bytes_accessed=read + wrote, transcendentals=0),
        compiler_params=pltpu.CompilerParams(vmem_limit_bytes=VMEM_BYTES),
    )(*args)


def to_right(value):
    size = lax.axis_size("tile")
    return lax.ppermute(value, "tile", [(i, (i + 1) % size) for i in range(size)])


def to_left(value):
    size = lax.axis_size("tile")
    return lax.ppermute(value, "tile", [(i, (i - 1) % size) for i in range(size)])


def with_partner(value, first):
    mem, tile = lax.axis_size("mem"), lax.axis_size("tile")
    pairs = []
    for m in range(mem):
        for t in range(tile):
            flip = 1 if (t % 2 == 0) == first else 3
            pairs.append((m * tile + t, (m ^ flip) * tile + t))
    return lax.ppermute(value, ("mem", "tile"), pairs)


def per_device(alpha, ensemble, innovation, precision, diffusivity):
    members, levels, columns, rows = alpha.shape
    slots = ensemble.shape[0]
    pairs = levels // 2
    work = members * levels * columns * rows * 10 * STEPS

    a_lo, a_hi = (rows8(alpha.shape, (1, 2), at) for at in (0, 2))
    c_lo, c_hi = (rows8(diffusivity.shape, (1, 2), at) for at in (0, 2))
    edge = f32(members + 2, pairs, TILE_ROWS, rows)
    edge_spec = block(edge.shape, (1, 1))
    head, tail = run(
        pack_controls, pairs, [a_lo, a_hi, c_lo, c_hi], [edge_spec] * 2, [edge] * 2, 0,
        alpha, alpha, diffusivity, diffusivity,
    )
    left = to_right(tail)
    right = to_left(head)

    ens_edge = f32(slots, members, pairs, TILE_ROWS, rows)
    ens_edge_spec = block(ens_edge.shape, (2, 1))
    ens_head, ens_tail = run(
        pack_ensemble, pairs, [block(ensemble.shape, (2, 2))], [ens_edge_spec] * 2, [ens_edge] * 2, 0,
        ensemble,
    )

    mid = f32(slots, levels, 16, rows)
    mid_spec = block(mid.shape, (1, 1))
    kept = f32(members, levels, TILE_ROWS, rows)
    kept_spec = block(kept.shape, (1, 1))
    kept2_spec = block(kept.shape, (1, 2))
    field = f32(*alpha.shape)
    field_spec = block(alpha.shape, (1, 1))
    field2_spec = block(alpha.shape, (1, 2))
    ens_spec = block(ensemble.shape, (2, 1))
    coeffs_spec = block(diffusivity.shape, (1, 1))
    part_mid, cells, fluxes = run(
        localize_interior, levels, [field_spec, ens_spec, coeffs_spec],
        [mid_spec, kept_spec, kept_spec], [mid, kept, kept], work, alpha, ensemble, diffusivity,
    )
    got_mid = with_partner(part_mid, True)

    rim = f32(slots, 2, pairs, TILE_ROWS, rows)
    rim_spec = block(rim.shape, (2, 1))
    part_rim = run(
        localize_edges, pairs,
        [edge_spec, edge_spec, kept2_spec, kept2_spec, c_lo, c_hi, ens_edge_spec, ens_edge_spec],
        rim_spec, rim, work // 3,
        left, right, cells, fluxes, diffusivity, diffusivity, ens_head, ens_tail,
    )
    got_rim = with_partner(part_rim, True)
    half_mid = part_mid + got_mid
    other_mid = with_partner(half_mid, False)
    half_rim = part_rim + got_rim
    other_rim = with_partner(half_rim, False)

    o_lo, o_hi = (rows8(innovation.shape, (1, 2), at) for at in (0, 2))
    p_edge = f32(members, pairs, TILE_ROWS, rows)
    p_edge_spec = block(p_edge.shape, (1, 1))
    rim_total = f32(slots, levels, TILE_ROWS, rows)
    rim_total_spec = block(rim_total.shape, (1, 1))
    rim_total2_spec = block(rim_total.shape, (1, 2))
    total_rim, p_head, p_tail = run(
        project_edges, pairs,
        [rim_spec, rim_spec, o_lo, o_hi, o_lo, o_hi, ens_edge_spec, ens_edge_spec],
        [rim_total2_spec, p_edge_spec, p_edge_spec], [rim_total, p_edge, p_edge], 0,
        half_rim, other_rim, innovation, innovation, precision, precision, ens_head, ens_tail,
    )
    p_left = to_right(p_tail)
    p_right = to_left(p_head)

    obs = f32(*innovation.shape)
    obs_spec = block(obs.shape, (1, 1))
    increment, inner, cells, fluxes = run(
        adjoint_interior, levels,
        [mid_spec, mid_spec, rim_total_spec, obs_spec, obs_spec, ens_spec, field_spec, coeffs_spec],
        [obs_spec, field_spec, kept_spec, kept_spec], [obs, field, kept, kept], work,
        half_mid, other_mid, total_rim, innovation, precision, ensemble, alpha, diffusivity,
    )

    gradient = run(
        adjoint_edges, pairs,
        [field2_spec, a_lo, a_hi, p_edge_spec, p_edge_spec, kept2_spec, kept2_spec,
         c_lo, c_hi, edge_spec, edge_spec],
        field2_spec, field, work // 3,
        inner, alpha, alpha, p_left, p_right, cells, fluxes,
        diffusivity, diffusivity, left, right,
    )
    return (gradient, increment)


def solution(mesh):
    in_specs = (
        P("mem", None, "tile", None),
        P(None, "mem", None, "tile", None),
        P(None, None, "tile", None),
        P(None, None, "tile", None),
        P(None, None, "tile", None),
    )
    out_specs = (P("mem", None, "tile", None), P(None, None, "tile", None))
    return jax.shard_map(
        per_device, mesh=mesh, in_specs=in_specs, out_specs=out_specs, check_vma=False
    )
```

```python
import functools
import math

import jax
import jax.numpy as jnp
from jax import lax
from jax.experimental import pallas as pl
from jax.experimental.pallas import tpu as pltpu
from jax.sharding import PartitionSpec as P

STEPS = 4
HALO = 4
TILE_ROWS = 8
VMEM_BYTES = 16 * 1024 * 1024
MOST_VMEM_BYTES = 48 * 1024 * 1024


def shifted(values, by, axis):
    return pltpu.roll(values, by % values.shape[axis], axis)


def low_half(shape):
    return lax.broadcasted_iota(jnp.int32, shape, len(shape) - 2) < HALO


def masked_rows(face):
    last = lax.broadcasted_iota(jnp.int32, face.shape, 1) == face.shape[1] - 1
    return jnp.where(last, 0.0, face)


def diffuse(fields, zonal, merid):
    rows = lax.broadcasted_iota(jnp.int32, (TILE_ROWS, zonal.shape[1]), 0)
    kept = [None] * len(fields)
    for sweep in range(STEPS):
        zonal_flux = [zonal * (shifted(f, -1, 0) - f) for f in fields]
        merid_flux = [merid * (shifted(f, -1, 1) - f) for f in fields]
        inward = [shifted(z, 1, 0) for z in zonal_flux]
        for i, f in enumerate(fields):
            cell = jnp.where(rows < HALO, f[:8], f[16:])
            flux = jnp.where(rows < HALO, zonal_flux[i][:8], inward[i][16:])
            if sweep:
                mine = (rows == sweep) | (rows == 7 - sweep)
                cell = jnp.where(mine, cell, kept[i][0])
                flux = jnp.where(mine, flux, kept[i][1])
            kept[i] = (cell, flux)
        fields = [
            (f + (z - w)) + (g - shifted(g, 1, 1))
            for f, z, w, g in zip(fields, zonal_flux, inward, merid_flux)
        ]
    return fields, kept


def window(outer, inner, by, side):
    if by == 0:
        return outer
    rows = lax.broadcasted_iota(jnp.int32, outer.shape, 0) % HALO
    if side == 0:
        return jnp.where(rows < HALO - by, shifted(outer, -by, 0), shifted(inner, HALO - by, 0))
    return jnp.where(rows >= by, shifted(outer, by, 0), shifted(inner, by - HALO, 0))


def edge_windows(outer, own, side):
    zonal_at = 0 if side == 0 else 1
    steps = []
    for step in range(STEPS):
        zonal = window(outer[0], own[0], step + zonal_at, side)
        merid = window(outer[1], own[1], step + 1, side)
        steps.append((zonal, masked_rows(merid)))
    return steps


def diffuse_edges(halos, kept, windows, side):
    rows = lax.broadcasted_iota(jnp.int32, halos[0].shape, 0) % HALO
    inward = -1 if side == 0 else 1
    newest = rows == (HALO - 1 if side == 0 else 0)
    outer = halos
    for step in range(STEPS):
        zonal, merid = windows[step]
        turn = -inward * (HALO - 1 - step)
        cells, flux_in = [], []
        for previous, (cell, flux) in zip(outer, kept):
            cells.append(jnp.where(newest, shifted(cell, turn, 0), shifted(previous, inward, 0)))
            flux_in.append(shifted(flux, turn, 0))
        merid_flux = [merid * (shifted(c, -1, 1) - c) for c in cells]
        after = []
        for previous, cell, flux, g in zip(outer, cells, flux_in, merid_flux):
            out_flux = zonal * (cell - previous if side == 0 else previous - cell)
            in_flux = jnp.where(newest, flux, shifted(out_flux, inward, 0))
            change = in_flux - out_flux if side == 0 else out_flux - in_flux
            after.append((cell + change) + (g - shifted(g, 1, 1)))
        outer = after
    return outer


def paired_heads(first, second):
    return jnp.where(low_half(first.shape), first, shifted(second, HALO, 0))


def paired_tails(first, second):
    return jnp.where(low_half(first.shape), shifted(first, HALO, 0), second)


def paired(first, second, side):
    return (paired_heads if side == 0 else paired_tails)(first, second)


def levels_of(left, right):
    low = low_half(left.shape)
    return (
        jnp.where(low, left, shifted(right, HALO, 0)),
        jnp.where(low, shifted(left, HALO, 0), right),
    )


def pack_controls(alpha, diffusivity, head, tail):
    members, pairs = alpha.shape[0], head.shape[1]
    for f in range(members + 2):
        source, at = (alpha, f) if f < members else (diffusivity, f - members)
        for p in range(pairs):
            first, second = 2 * p, 2 * p + 1
            head[f, p] = paired_heads(source[at, first, :8], source[at, second, :8])
            tail[f, p] = paired_tails(source[at, first, 16:], source[at, second, 16:])


def localize_interior(alpha, ensemble, coeffs, out, cells, fluxes, rims):
    members, levels = alpha.shape[:2]
    low = low_half((TILE_ROWS, alpha.shape[3]))

    def one(i, carry):
        fields = [alpha[m, i] for m in range(members)]
        fields, kept = diffuse(fields, coeffs[0, i], masked_rows(coeffs[1, i]))
        for m, (cell, flux) in enumerate(kept):
            cells[m, i] = cell
            fluxes[m, i] = flux
        for t in range(2):
            for m in range(members):
                scale = ensemble[t, m, i].astype(jnp.float32)
                rims[t, m, i] = jnp.where(low, scale[:8], scale[16:])
                total = scale * fields[m] if m == 0 else total + scale * fields[m]
            out[t, i, :8] = total[8:16]
            out[t, i, 8:] = jnp.where(low, total[16:], total[:8])
        return carry

    lax.fori_loop(0, levels, one, 0)


def two(ref, pair):
    ahead = (slice(None),) * (len(ref.shape) - 3)
    return ref.at[ahead + (pl.ds(2 * pair, 2),)]


def edges_of(halos, cells, fluxes, coeffs, outer, side):
    members = cells.shape[0]
    rows = slice(0, 8) if side == 0 else slice(16, 24)
    own = [paired(coeffs[f, 0, rows], coeffs[f, 1, rows], side) for f in range(2)]
    windows = edge_windows([outer[members], outer[members + 1]], own, side)
    kept = [
        tuple(paired(k[m, 0], k[m, 1], side) for k in (cells, fluxes)) for m in range(members)
    ]
    return diffuse_edges([halos[m] for m in range(members)], kept, windows, side)


def localize_edges(left, right, cells, fluxes, coeffs, rims, out):
    members = cells.shape[0]

    def one(pair, carry):
        scale, rim = two(rims, pair), two(out, pair)
        kept = two(cells, pair), two(fluxes, pair), two(coeffs, pair)
        sides = [
            edges_of(outer.at[:, pair], *kept, outer.at[:, pair], side)
            for side, outer in enumerate((left, right))
        ]
        edges = [levels_of(sides[0][m], sides[1][m]) for m in range(members)]
        for j in range(2):
            for t in range(2):
                for m in range(members):
                    term = scale[t, m, j] * edges[m][j]
                    total = term if m == 0 else total + term
                rim[t, j] = total
        return carry

    lax.fori_loop(0, left.shape[1], one, 0)


def project_edges(mine, other, innovation, precision, rims, rim, head, tail):
    members = rims.shape[1]
    low = low_half(mine.shape[2:])

    def one(pair, carry):
        scale, out = two(rims, pair), two(rim, pair)
        parts = [two(ref, pair) for ref in (mine, other, innovation, precision)]
        edges = []
        for j in range(2):
            edge = []
            for t in range(2):
                total = parts[0][t, j] + parts[1][t, j]
                out[t, j] = total
                seen, trust = (jnp.where(low, p[t, j, :8], p[t, j, 16:]) for p in parts[2:])
                edge.append(trust * (total - seen))
            edges.append(edge)
        for m in range(members):
            first, second = (
                scale[0, m, j] * edges[j][0] + scale[1, m, j] * edges[j][1] for j in range(2)
            )
            head[m, pair] = paired_heads(first, second)
            tail[m, pair] = paired_tails(first, second)
        return carry

    lax.fori_loop(0, head.shape[1], one, 0)


def adjoint_interior(
    mine, other, rim, innovation, precision, ensemble, alpha, coeffs,
    increment, inner, cells, fluxes,
):
    members, levels = alpha.shape[:2]
    low = low_half((TILE_ROWS, alpha.shape[3]))

    def one(i, carry):
        scale, control, face = ensemble.at[:, :, i], alpha.at[:, i], coeffs.at[:, i]
        out = [ref.at[:, i] for ref in (inner, cells, fluxes)]
        weight = []
        for t in range(2):
            middle = mine[t, i] + other[t, i]
            edge, rest = rim[t, i], middle[8:]
            total = jnp.concatenate(
                [jnp.where(low, edge, rest), middle[:8], jnp.where(low, rest, edge)], axis=0
            )
            increment[t, i] = total
            weight.append(precision[t, i] * (total - innovation[t, i]))
        projected = [
            scale[0, m].astype(jnp.float32) * weight[0] + scale[1, m].astype(jnp.float32) * weight[1]
            for m in range(members)
        ]
        fields, kept = diffuse(projected, face[0], masked_rows(face[1]))
        for m, (cell, flux) in enumerate(kept):
            out[1][m] = cell
            out[2][m] = flux
            out[0][m] = control[m] + fields[m]
        return carry

    lax.fori_loop(0, levels, one, 0)


def adjoint_edges(
    inner, alpha, p_left, p_right, cells, fluxes, coeffs, left, right, increment,
    gradient, whole_increment,
):
    pair = pl.program_id(0)
    members = alpha.shape[0]
    low = low_half((TILE_ROWS, alpha.shape[3]))
    kept = two(cells, pair), two(fluxes, pair), two(coeffs, pair)
    inside, control, total = two(inner, pair), two(alpha, pair), two(increment, pair)
    sides = [
        edges_of(halos.at[:, pair], *kept, outer.at[:, pair], side)
        for side, (halos, outer) in enumerate(((p_left, left), (p_right, right)))
    ]
    for m in range(members):
        for j, edge in enumerate(levels_of(sides[0][m], sides[1][m])):
            gradient[m, j, :8] = jnp.where(low, control[m, j, :8] + edge, inside[m, j, :8])
            gradient[m, j, 8:16] = inside[m, j, 8:16]
            gradient[m, j, 16:] = jnp.where(low, inside[m, j, 16:], control[m, j, 16:] + edge)
    for t in range(2):
        for j in range(2):
            whole_increment[t, j] = total[t, j]


def f32(*shape):
    return jax.ShapeDtypeStruct(shape, jnp.float32)


def run(kernel, out_shape, flops, *args, vmem=VMEM_BYTES, **options):
    read = sum(a.size * a.dtype.itemsize for a in args)
    wrote = sum(4 * math.prod(s.shape) for s in out_shape)
    whole = pl.BlockSpec(memory_space=pltpu.VMEM)
    if "grid_spec" not in options:
        options = {"in_specs": [whole] * len(args), "out_specs": [whole] * len(out_shape)} | options
    return pl.pallas_call(
        kernel,
        out_shape=out_shape,
        cost_estimate=pl.CostEstimate(flops=flops, bytes_accessed=read + wrote, transcendentals=0),
        compiler_params=pltpu.CompilerParams(vmem_limit_bytes=vmem),
        **options,
    )(*args)


def in_vmem(value):
    return pltpu.with_memory_space_constraint(value, pltpu.VMEM)


def to_right(value):
    size = lax.axis_size("tile")
    return lax.ppermute(value, "tile", [(i, (i + 1) % size) for i in range(size)])


def to_left(value):
    size = lax.axis_size("tile")
    return lax.ppermute(value, "tile", [(i, (i - 1) % size) for i in range(size)])


def with_partner(value, first):
    mem, tile = lax.axis_size("mem"), lax.axis_size("tile")
    pairs = []
    for m in range(mem):
        for t in range(tile):
            flip = 1 if (t % 2 == 0) == first else 3
            pairs.append((m * tile + t, (m ^ flip) * tile + t))
    return lax.ppermute(value, ("mem", "tile"), pairs)


def per_device(alpha, ensemble, innovation, precision, diffusivity):
    members, levels, columns, rows = alpha.shape
    slots = ensemble.shape[0]
    pairs = levels // 2
    work = members * levels * columns * rows * 10 * STEPS

    edge = pltpu.VMEM((members + 2, pairs, TILE_ROWS, rows), jnp.float32)
    head, tail = run(pack_controls, [edge, edge], 0, alpha, diffusivity)
    left = in_vmem(to_right(tail))
    right = in_vmem(to_left(head))

    kept = f32(members, levels, TILE_ROWS, rows)
    part_mid, cells, fluxes, rims = run(
        localize_interior,
        [f32(slots, levels, 16, rows), kept, kept, f32(slots, members, levels, TILE_ROWS, rows)],
        work, alpha, ensemble, diffusivity, vmem=MOST_VMEM_BYTES,
    )
    got_mid = with_partner(part_mid, True)
    (part_rim,) = run(
        localize_edges, [f32(slots, levels, TILE_ROWS, rows)], work // 3,
        left, right, cells, fluxes, diffusivity, rims,
    )
    got_rim = with_partner(part_rim, True)
    half_mid = part_mid + got_mid
    other_mid = with_partner(half_mid, False)
    half_rim = part_rim + got_rim
    other_rim = with_partner(half_rim, False)

    p_edge = f32(members, pairs, TILE_ROWS, rows)
    rim, p_head, p_tail = run(
        project_edges, [f32(slots, levels, TILE_ROWS, rows), p_edge, p_edge], 0,
        half_rim, other_rim, innovation, precision, rims,
    )
    p_left = to_right(p_tail)
    p_right = to_left(p_head)

    obs, field = f32(*innovation.shape), f32(*alpha.shape)
    increment, inner, cells, fluxes = run(
        adjoint_interior, [obs, field, kept, kept], work,
        half_mid, other_mid, rim, innovation, precision, ensemble, alpha, diffusivity,
    )
    args = (inner, alpha, p_left, p_right, cells, fluxes, diffusivity, left, right, increment)
    return tuple(
        run(
            adjoint_edges, [field, obs], work // 3, *args,
            grid=(pairs,),
            out_specs=[
                pl.BlockSpec((members, 2, columns, rows), lambda i: (0, i, 0, 0)),
                pl.BlockSpec((slots, 2, columns, rows), lambda i: (0, i, 0, 0)),
            ],
        )
    )


def solution(mesh):
    in_specs = (
        P("mem", None, "tile", None),
        P(None, "mem", None, "tile", None),
        P(None, None, "tile", None),
        P(None, None, "tile", None),
        P(None, None, "tile", None),
    )
    out_specs = (P("mem", None, "tile", None), P(None, None, "tile", None))
    return jax.shard_map(
        per_device, mesh=mesh, in_specs=in_specs, out_specs=out_specs, check_vma=False
    )
```
